32 devices in a mesh: groups: 2 (over x), tensor: 8 (over z, y), req: 2 (over core).
Axes of the slice: x: 2, y: 2, z: 4, core: 2. Of those that a mesh axis runs over, the one named last changes fastest.
Arguments:
- queries: bfloat16 [32, 64, 128], P(('groups', 'req'), 'tensor'), parts along dimension 0, may hold values from -48 to 48
- key_cache: bfloat16 [32, 4096, 4, 128], P(('groups', 'req'), 'tensor'), parts along dimension 0, may hold values from -16 to 16
- value_cache: bfloat16 [32, 4096, 4, 128], P(('groups', 'req'), 'tensor'), parts along dimension 0, may hold values from -6 to 6
- fresh_pair: bfloat16 [32, 2, 4, 128], P(('groups', 'req')), parts along dimension 0, may hold values from -12 to 12
- lengths: int32 [32], P(('groups', 'req')), parts along dimension 0, may hold values from 256 to 4096, as said below
- out_weight: bfloat16 [8192, 16384], P('tensor'), may hold values from -0.09375 to 0.09375
- residual: bfloat16 [32, 16384], P(('groups', 'req'), 'tensor'), parts along dimension 0, may hold values from -40 to 40
- norm_gain: bfloat16 [16384], replicated, may hold values from 0.5 to 1.5
- partial_exponents: int32 [8, 32, 128], P('tensor', ('groups', 'req')), parts along dimension 1, may hold values from -13 to -9
- normed_exponents: int32 [32, 128], P(('groups', 'req')), parts along dimension 0, may hold values from -8 to -5
Outputs:
- hidden_state: bfloat16 [32, 16384], P(('groups', 'req'), 'tensor'), parts along dimension 0
- normed: bfloat16 [32, 16384], P(('groups', 'req')), parts along dimension 0
The draws below stay inside these ranges and needn't reach their ends.
There are 2 independent parts, one for each index of `groups`. The reference program is written for one: setup_inputs(seed, part) draws one part's arguments, and reference() takes and returns one part's arrays. A program takes and returns all parts, laid end to end along the dimension named above; an argument that names none is the same for every part. Nothing has to cross between parts.
Inputs may be any that keep to these rules, and one draw needn't show every extreme that they name: Row r holds keys at cache positions below lengths[r]; some row of each draw has all 4096.
All inputs are finite; a program needn't handle non-finite values.
Results may differ from the reference program's by a relative error of at most 0.0075.
Values may be sent and summed in bfloat16 or wider, within the bound.
A program may use at most 192 MiB of HBM per device.

```python
import math
import jax
import jax.numpy as jnp
from jax import lax

D = 16384
HD = 128
HQW = 64
KVW = 4
LEN = 4096
BLOCK = 128
ROWS = 16
N_TENSOR = 8


def row_section(key):
    offset = jax.random.randint(jax.random.fold_in(key, 202), (), 0, 4)
    return ((jnp.arange(ROWS) + offset) % 4).astype(jnp.int32)


def draw_queries(key, part):
    key = jax.random.fold_in(key, 1)
    values = jnp.clip(2.5 * jax.random.normal(key, (ROWS, HQW, HD), jnp.float32), -10.0, 10.0)
    return values.astype(jnp.bfloat16)


def draw_key_cache(key, part):
    key = jax.random.fold_in(key, 2)
    values = jnp.clip(jax.random.normal(key, (ROWS, LEN, KVW, HD), jnp.float32), -6.0, 6.0)
    return values.astype(jnp.bfloat16)


def draw_lengths(key, part):
    sections = row_section(key)
    key = jax.random.fold_in(key, 3)
    spans = jax.random.randint(key, (ROWS,), LEN // 16, LEN + 1)
    long_spans = jax.random.randint(jax.random.fold_in(key, 5), (ROWS,), LEN // 2 + 2, LEN + 1)
    spans = jnp.where(sections != 0, long_spans, spans)
    chosen = jax.random.randint(jax.random.fold_in(key, 7), (), 0, ROWS)
    return jnp.where(jnp.arange(ROWS) == chosen, LEN, spans).astype(jnp.int32)


def draw_residual(key, part):
    key = jax.random.fold_in(key, 4)
    bumps = jax.random.uniform(jax.random.fold_in(key, 11), (D // BLOCK,), jnp.float32, -0.6, 0.6)
    base = jnp.clip(jax.random.normal(jax.random.fold_in(key, 12), (ROWS, D), jnp.float32), -4.0, 4.0)
    row_log = jax.random.uniform(jax.random.fold_in(key, 13), (ROWS,), jnp.float32, math.log(0.3), math.log(3.0))
    slope = math.log(3.0)
    columns = 0.5 * jnp.exp(slope * jnp.arange(D, dtype=jnp.float32) / D + jnp.repeat(bumps, BLOCK))
    values = base * jnp.exp(row_log)[:, None] * columns[None, :]
    return values.astype(jnp.bfloat16)


def set_ends(array, rng, low, largest):
    extent = array.shape
    spot = [jax.random.randint(jax.random.fold_in(rng, axis), (), 0, extent[axis]) for axis in range(len(extent))]
    array = array.at[tuple(spot)].set(low)
    longest = extent.index(max(extent))
    spot[longest] = (spot[longest] + 1) % extent[longest]
    return array.at[tuple(spot)].set(largest)


def spiked(values, rng, source, target, blocks, factor):
    def block_of(axis_at):
        return (jnp.arange(values.shape[axis_at]) // (values.shape[axis_at] // blocks)).reshape((-1,) + (1,) * (values.ndim - 1 - axis_at))

    near = jax.random.permutation(rng, blocks)[block_of(target)]
    other_side = (block_of(target) + blocks // 2) % blocks
    return jnp.where((block_of(source) == near) | (block_of(source) == other_side), factor * values, values)


def block_levels(stream_key, dims, split, low, largest):
    gain, own = 1.0, jax.random.fold_in(stream_key, 6)
    for axis_at, shards_of in split:
        draws = jnp.exp(jax.random.uniform(jax.random.fold_in(own, axis_at), (shards_of,), jnp.float32, low / len(split), largest / len(split)))
        gain = gain * jnp.repeat(draws, dims[axis_at] // shards_of).reshape([-1 if axis == axis_at else 1 for axis in range(len(dims))])
    return gain


def normal_values(key, shape, width, reach, split=(), held_as=jnp.bfloat16):
    drawn = jax.random.normal(key, shape, jnp.float32) * width
    if len(split) > 0:
        drawn = block_levels(key, shape, split, -0.22, 0.18) * drawn
    return jnp.clip(drawn, min=-reach, max=reach).astype(held_as)


def heavy_noise(key, extent, deviation, bound, split, heavy, kind=jnp.bfloat16):
    array = deviation * jax.random.normal(key, extent, jnp.float32)
    if split:
        array = array * block_levels(key, extent, split, -0.22, 0.18)
    return jnp.clip(spiked(array, jax.random.fold_in(key, 3), *heavy), -bound, bound).astype(kind)


def setup_inputs(seed: int = 0, part: int = 0) -> dict:
    arg_keys = jax.random.split(jax.random.key(seed), 11)
    part_keys = jax.random.split(jax.random.fold_in(arg_keys[10], part), 11)
    return {
        "queries": draw_queries(jax.random.fold_in(jax.random.fold_in(arg_keys[10], part), 71), part),
        "key_cache": draw_key_cache(jax.random.fold_in(jax.random.fold_in(arg_keys[10], part), 71), part),
        "value_cache": normal_values(part_keys[2], (ROWS, LEN, KVW, HD), 1.0, 6.0, ((0, 2), (1, 8))),
        "fresh_pair": normal_values(part_keys[3], (ROWS, 2, KVW, HD), 2.5, 12.0, ((0, 2),)),
        "lengths": draw_lengths(jax.random.fold_in(jax.random.fold_in(arg_keys[10], part), 71), part),
        "out_weight": heavy_noise(arg_keys[5], (HQW * HD, D), (HQW * HD) ** -0.5, 0.09375, ((0, 8),), (0, 1, 8, 2.0)),
        "residual": draw_residual(jax.random.fold_in(jax.random.fold_in(arg_keys[10], part), 71), part),
        "norm_gain": jnp.clip(1.0 + 0.1 * jax.random.normal(arg_keys[7], (D,), jnp.float32), 0.5, 1.5).astype(jnp.bfloat16),
        "partial_exponents": set_ends(jax.random.randint(part_keys[8], (N_TENSOR, ROWS, D // BLOCK), -13, -8), jax.random.fold_in(part_keys[8], 1), -13, (-8) - 1).astype(jnp.int32),
        "normed_exponents": set_ends(jax.random.randint(part_keys[9], (ROWS, D // BLOCK), -8, -4), jax.random.fold_in(part_keys[9], 1), -8, (-4) - 1).astype(jnp.int32),
    }


def power_two(exponents):
    result = jnp.zeros(exponents.shape, jnp.float32)
    for exponent in range(-24, 25):
        result = result + jnp.where(exponents == exponent, jnp.float32(2.0 ** exponent), jnp.float32(0.0))
    return result

def code_blocks(values, exponents):
    row_count, full_width = values.shape
    blocks = exponents.shape[1]
    shaped = values.reshape(row_count, blocks, full_width // blocks)
    dequant = jnp.clip(shaped * power_two(-exponents)[:, :, None], -448.0, 448.0).astype(jnp.bfloat16)
    dequant = lax.optimization_barrier(dequant)
    return (dequant.astype(jnp.float32) * power_two(exponents)[:, :, None]).reshape(row_count, full_width)

def finish_norm(state_rows, norm_gain, exponents):
    values = state_rows.astype(jnp.float32)
    mean_square = lax.optimization_barrier(jnp.mean(values * values, axis=-1, keepdims=True))
    scaled = values * lax.rsqrt(mean_square + 1e-05) * norm_gain.astype(jnp.float32)
    return code_blocks(scaled, exponents).astype(jnp.bfloat16)

def reference(queries, key_cache, value_cache, fresh_pair, lengths, out_weight, residual, norm_gain, partial_exponents, normed_exponents):
    row_count, head_count, head_size = queries.shape
    kv_count = key_cache.shape[2]
    per_group = head_count // kv_count
    factor = head_size ** (-0.5)
    grouped = queries.astype(jnp.float32).reshape(row_count, kv_count, per_group, head_size)
    scores = jnp.einsum('rgnd,rpgd->rgnp', grouped, key_cache.astype(jnp.float32)) * factor
    usable = (jnp.arange(LEN)[None, :] < lengths[:, None])[:, None, None, :]
    fresh_score = jnp.einsum('rgnd,rgd->rgn', grouped, fresh_pair[:, 0].astype(jnp.float32)) * factor
    highest = jnp.maximum(lax.optimization_barrier(jnp.max(jnp.where(usable, scores, -1e+30), axis=-1)), fresh_score)
    weights = jnp.where(usable, jnp.exp(scores - highest[..., None]), 0.0)
    own_weight = jnp.exp(fresh_score - highest)
    weight_sum = lax.optimization_barrier(jnp.sum(weights, axis=-1)) + own_weight
    mixture = jnp.einsum('rgnp,rpgd->rgnd', weights, value_cache.astype(jnp.float32))
    mixture = mixture + own_weight[..., None] * fresh_pair[:, 1].astype(jnp.float32)[:, :, None, :]
    attended = (mixture / weight_sum[..., None]).reshape(row_count, head_count * head_size).astype(jnp.bfloat16)
    span_width = head_count * head_size // N_TENSOR

    def add_term(position, running):
        start = (position * span_width).astype(jnp.int32)
        piece_cols = lax.dynamic_slice_in_dim(attended, start, span_width, 1)
        weight_rows = lax.dynamic_slice_in_dim(out_weight, start, span_width, 0)
        partial_value = jnp.dot(piece_cols, weight_rows, preferred_element_type=jnp.float32)
        exponents = lax.dynamic_index_in_dim(partial_exponents, position.astype(jnp.int32), axis=0, keepdims=False)
        return running + code_blocks(partial_value, exponents)
    attention_sum = lax.fori_loop(jnp.int32(0), jnp.int32(N_TENSOR), add_term, jnp.zeros((row_count, D), jnp.float32))
    hidden_state = (residual.astype(jnp.float32) + attention_sum).astype(jnp.bfloat16)
    return (hidden_state, finish_norm(hidden_state, norm_gain, normed_exponents))
```

```python
import functools
import math

import jax
import jax.numpy as jnp
from jax import lax
from jax.experimental import pallas as pl
from jax.experimental.pallas import tpu as pltpu
from jax.sharding import PartitionSpec as P

MESH = pl.DeviceIdType.MESH
LOW = -1e30


def power_two(exponents):
    shifted = exponents + 32
    result = jnp.full(exponents.shape, 2.0**-32, jnp.float32)
    for bit in range(6):
        is_set = (lax.shift_right_logical(shifted, bit) & 1) == 1
        result = result * jnp.where(is_set, jnp.float32(2.0 ** (2**bit)), jnp.float32(1.0))
    return result


def kernel(
    n,
    own_heads,
    kv_count,
    lengths_ref,
    q_hbm,
    k_hbm,
    v_hbm,
    fresh_hbm,
    w_hbm,
    residual_hbm,
    gain_hbm,
    pexp_hbm,
    nexp_hbm,
    hidden_ref,
    normed_ref,
    kbuf,
    vbuf,
    wbuf,
    qbuf,
    q32,
    fresh,
    residual,
    gain,
    pexp,
    nexp,
    groups_at,
    plim,
    nlim,
    mix32,
    mix_out,
    mix_in,
    stat_own,
    stat_in,
    att,
    rs_out,
    rs_in,
    ag,
    k_sem,
    v_sem,
    w_sem,
    small_sem,
    own_sem,
    send_sem,
    recv_sem,
):
    me = lax.axis_index("tensor")
    rows = kbuf.shape[0]
    spots = kbuf.shape[1]
    head_size = kbuf.shape[2]
    heads = n * own_heads
    per_group = heads // kv_count
    share = wbuf.shape[2]
    half = share // 2
    block = 128
    blocks = share // block
    c = head_size ** (-0.5) / math.log(2.0)

    def partner(k):
        return lax.rem(me + k, n)

    barrier = pltpu.get_barrier_semaphore()

    @pl.loop(1, n)
    def _(k):
        pl.semaphore_signal(barrier, inc=1, device_id={"tensor": partner(k)}, device_id_type=MESH)

    own_q = pltpu.make_async_copy(q_hbm, qbuf.at[me], own_sem)
    own_q.start()
    small = [
        pltpu.make_async_copy(fresh_hbm, fresh, small_sem.at[0]),
        pltpu.make_async_copy(pexp_hbm, pexp, small_sem.at[1]),
        pltpu.make_async_copy(nexp_hbm, nexp, small_sem.at[2]),
        pltpu.make_async_copy(gain_hbm, gain, small_sem.at[3]),
        pltpu.make_async_copy(residual_hbm, residual, small_sem.at[4]),
    ]
    for copy in small:
        copy.start()

    def k_copy(r):
        return pltpu.make_async_copy(k_hbm.at[r], kbuf.at[r], k_sem.at[r])

    def v_copy(r):
        return pltpu.make_async_copy(v_hbm.at[r], vbuf.at[r], v_sem.at[r])

    def w_copy(j):
        return pltpu.make_async_copy(
            w_hbm.at[:, pl.ds(pl.multiple_of(j * share, share), share)], wbuf.at[j], w_sem.at[j]
        )

    for r in range(rows):
        k_copy(r).start()
        v_copy(r).start()

    @pl.loop(0, n)
    def _(k):
        w_copy(partner(k + 1)).start()

    own_q.wait()
    pl.semaphore_wait(barrier, n - 1)

    def remote(phase, src, dst, to, frm):
        return pltpu.make_async_remote_copy(
            src_ref=src,
            dst_ref=dst,
            send_sem=send_sem.at[phase, to],
            recv_sem=recv_sem.at[phase, frm],
            device_id={"tensor": to},
            device_id_type=MESH,
        )

    @pl.loop(1, n)
    def _(k):
        remote(0, qbuf.at[me], qbuf.at[me], partner(k), me).start()

    columns = lax.broadcasted_iota(jnp.int32, (heads, spots), 1)
    head_of = lax.broadcasted_iota(jnp.int32, (heads, spots), 0)
    groups_at[...] = jnp.where(
        lax.rem(columns, kv_count) == lax.div(head_of, per_group), columns, 1 << 24
    )
    for copy in small:
        copy.wait()
    plimits = 448.0 * power_two(pexp[0])
    nlimits = 448.0 * power_two(nexp[...])
    for b in range(n * blocks):
        plim[b] = jnp.broadcast_to(plimits[:, b : b + 1], (rows, block))
        nlim[b] = jnp.broadcast_to(nlimits[:, b : b + 1], (rows, block))

    @pl.loop(1, n)
    def _(k):
        src = partner(k)
        remote(0, qbuf.at[src], qbuf.at[src], src, src).wait_recv()

    for t in range(n):
        q32[:, t * own_heads : (t + 1) * own_heads, :] = (
            qbuf[t].astype(jnp.float32).reshape(rows, own_heads, head_size)
        )

    @pl.loop(0, rows)
    def _(r):
        q = q32[r]
        fresh_row = fresh[r].astype(jnp.float32)
        fresh_key = jnp.concatenate(
            [
                jnp.broadcast_to(fresh_row[g : g + 1], (per_group, head_size))
                for g in range(kv_count)
            ],
            axis=0,
        )
        fresh_value = jnp.concatenate(
            [
                jnp.broadcast_to(fresh_row[kv_count + g : kv_count + g + 1], (per_group, head_size))
                for g in range(kv_count)
            ],
            axis=0,
        )
        fresh_score = jnp.sum(q * fresh_key, axis=1, keepdims=True)
        fresh_score = jnp.where(me == 0, fresh_score, LOW)
        k_copy(r).wait()
        scores = lax.dot_general(
            q.astype(jnp.bfloat16),
            kbuf[r],
            (((1,), (1,)), ((), ())),
            preferred_element_type=jnp.float32,
        )
        limit = lengths_ref[r] * kv_count - me * spots
        scores = jnp.where(groups_at[...] < limit, scores, LOW)
        top = jnp.maximum(jnp.max(scores, axis=1, keepdims=True), fresh_score)
        weights = jnp.exp2((scores - top) * c)
        own_weight = jnp.exp2((fresh_score - top) * c)
        total = jnp.sum(weights, axis=1, keepdims=True) + own_weight
        v_copy(r).wait()
        mix = jnp.dot(
            weights.astype(jnp.bfloat16), vbuf[r], preferred_element_type=jnp.float32
        )
        mix = mix + own_weight * fresh_value
        mix32[pl.ds(r, heads, stride=rows), :] = mix
        stats = jnp.concatenate(
            [
                jnp.broadcast_to(top, (heads, 2 * heads)),
                jnp.broadcast_to(total, (heads, 2 * heads)),
            ],
            axis=0,
        )
        stat_own[pl.ds(r, 1), :] = jnp.transpose(stats)[0:1]

    piece = own_heads * rows
    for t in range(n):
        mix_out[t] = mix32[t * piece : (t + 1) * piece, :].astype(jnp.bfloat16)

    @pl.loop(1, n)
    def _(k):
        dst = partner(k)
        remote(2, stat_own, stat_in.at[me], dst, me).start()
        remote(1, mix_out.at[dst], mix_in.at[me], dst, me).start()

    stat_in[me] = stat_own[...]
    mix_in[me] = mix_out[me]

    @pl.loop(1, n)
    def _(k):
        src = partner(k)
        remote(2, stat_own, stat_in.at[src], src, src).wait_recv()
        remote(1, mix_out.at[src], mix_in.at[src], src, src).wait_recv()

    tops = [stat_in[s] for s in range(n)]
    highest = functools.reduce(jnp.maximum, tops)
    scales = [jnp.exp2((top - highest) * c) for top in tops]
    weight_sum = sum(
        pltpu.roll(tops[s], heads, 1) * scales[s] for s in range(n)
    )
    shift = lax.rem(2 * heads - me * own_heads, 2 * heads)
    inverse = 1.0 / weight_sum
    scales = [pltpu.roll(scale * inverse, shift, 1) for scale in scales]
    arrived = [mix_in[s].astype(jnp.float32) for s in range(n)]
    pieces = []
    for h in range(own_heads):
        pieces.append(
            sum(
                arrived[s][h * rows : (h + 1) * rows] * scales[s][:, h : h + 1] for s in range(n)
            )
        )
    att[...] = jnp.concatenate(pieces, axis=1).astype(jnp.bfloat16)

    step = min(512, half)

    def project(j):
        w_copy(j).wait()
        out = []
        for at in range(0, share, step):
            value = jnp.dot(
                att[...], wbuf[j, :, at : at + step], preferred_element_type=jnp.float32
            )
            limit = jnp.concatenate(
                [plim[j * blocks + at // block + b] for b in range(step // block)], axis=1
            )
            out.append(jnp.clip(value, -limit, limit))
        left = jnp.concatenate(out[: len(out) // 2], axis=1)
        right = jnp.concatenate(out[len(out) // 2 :], axis=1)
        return jnp.concatenate([left, right], axis=0).astype(jnp.bfloat16)

    @pl.loop(1, n)
    def _(k):
        dst = partner(k)
        rs_out[dst] = project(dst)
        remote(3, rs_out.at[dst], rs_in.at[me], dst, me).start()

    rs_in[me] = project(me)
    own = residual[...].astype(jnp.float32)
    total = jnp.concatenate([own[:, :half], own[:, half:]], axis=0)

    @pl.loop(1, n)
    def _(k):
        src = partner(k)
        remote(3, rs_out.at[src], rs_in.at[src], src, src).wait_recv()

    summed = rs_in[0].astype(jnp.float32)
    for s in range(1, n):
        summed = summed + rs_in[s].astype(jnp.float32)
    ag[me] = (total + summed).astype(jnp.bfloat16)

    @pl.loop(1, n)
    def _(k):
        remote(4, ag.at[me], ag.at[me], partner(k), me).start()

    state = ag[me].astype(jnp.float32)
    hidden_ref[...] = jnp.concatenate([state[:rows], state[rows:]], axis=1).astype(jnp.bfloat16)

    @pl.loop(1, n)
    def _(k):
        src = partner(k)
        remote(4, ag.at[src], ag.at[src], src, src).wait_recv()

    squares = jnp.zeros((2 * rows, half), jnp.float32)
    for s in range(n):
        value = ag[s].astype(jnp.float32)
        squares = squares + value * value
    squares = jnp.sum(squares, axis=1, keepdims=True)
    squares = squares[:rows] + squares[rows:]
    gains = gain[...].astype(jnp.float32)
    root = lax.rsqrt(squares / (n * share) + 1e-05)
    for s in range(n):
        value = ag[s].astype(jnp.float32)
        out = []
        for b in range(blocks):
            side, at = divmod(b * block, half)
            part = value[side * rows : (side + 1) * rows, at : at + block]
            index = s * blocks + b
            scaled = part * root * gains[index : index + 1, :]
            out.append(jnp.clip(scaled, -nlim[index], nlim[index]))
        normed_ref[:, s * share : (s + 1) * share] = jnp.concatenate(out, axis=1).astype(
            jnp.bfloat16
        )

    @pl.loop(1, n)
    def _(k):
        dst = partner(k)
        remote(0, qbuf.at[me], qbuf.at[me], dst, me).wait_send()
        remote(1, mix_out.at[dst], mix_in.at[me], dst, me).wait_send()
        remote(2, stat_own, stat_in.at[me], dst, me).wait_send()
        remote(3, rs_out.at[dst], rs_in.at[me], dst, me).wait_send()
        remote(4, ag.at[me], ag.at[me], dst, me).wait_send()


def on_device(
    n,
    queries,
    key_cache,
    value_cache,
    fresh_pair,
    lengths,
    out_weight,
    residual,
    norm_gain,
    partial_exponents,
    normed_exponents,
):
    rows, own_heads, head_size = queries.shape
    positions, kv_count = key_cache.shape[1:3]
    spots = positions * kv_count
    heads = n * own_heads
    depth, width = out_weight.shape
    share = width // n
    half = share // 2
    all_blocks = normed_exponents.shape[1]
    block = width // all_blocks
    piece = rows * own_heads
    anywhere = pl.BlockSpec(memory_space=pl.ANY)
    in_vmem = pl.BlockSpec(memory_space=pltpu.VMEM)
    bf16, f32 = jnp.bfloat16, jnp.float32
    dma = pltpu.SemaphoreType.DMA
    return pl.pallas_call(
        functools.partial(kernel, n, own_heads, kv_count),
        out_shape=(
            jax.ShapeDtypeStruct((rows, share), bf16),
            jax.ShapeDtypeStruct((rows, width), bf16),
        ),
        in_specs=[pl.BlockSpec(memory_space=pltpu.SMEM)] + [anywhere] * 9,
        out_specs=(in_vmem, in_vmem),
        scratch_shapes=[
            pltpu.VMEM((rows, spots, head_size), bf16),
            pltpu.VMEM((rows, spots, head_size), bf16),
            pltpu.VMEM((n, depth, share), bf16),
            pltpu.VMEM((n, piece, head_size), bf16),
            pltpu.VMEM((rows, heads, head_size), f32),
            pltpu.VMEM((rows, 2 * kv_count, head_size), bf16),
            pltpu.VMEM((rows, share), bf16),
            pltpu.VMEM((all_blocks, block), bf16),
            pltpu.VMEM((1, rows, all_blocks), jnp.int32),
            pltpu.VMEM((rows, all_blocks), jnp.int32),
            pltpu.VMEM((heads, spots), jnp.int32),
            pltpu.VMEM((all_blocks, rows, block), f32),
            pltpu.VMEM((all_blocks, rows, block), f32),
            pltpu.VMEM((heads * rows, head_size), f32),
            pltpu.VMEM((n, piece, head_size), bf16),
            pltpu.VMEM((n, piece, head_size), bf16),
            pltpu.VMEM((rows, 2 * heads), f32),
            pltpu.VMEM((n, rows, 2 * heads), f32),
            pltpu.VMEM((rows, depth), bf16),
            pltpu.VMEM((n, 2 * rows, half), bf16),
            pltpu.VMEM((n, 2 * rows, half), bf16),
            pltpu.VMEM((n, 2 * rows, half), bf16),
            dma((rows,)),
            dma((rows,)),
            dma((n,)),
            dma((5,)),
            dma,
            dma((5, n)),
            dma((5, n)),
        ],
        compiler_params=pltpu.CompilerParams(
            collective_id=0, has_side_effects=True, vmem_limit_bytes=60 * 2**20
        ),
    )(
        lengths,
        queries.reshape(piece, head_size),
        key_cache.reshape(rows, spots, head_size),
        value_cache.reshape(rows, spots, head_size),
        fresh_pair.reshape(rows, 2 * kv_count, head_size),
        out_weight,
        residual,
        norm_gain.reshape(all_blocks, block),
        partial_exponents,
        normed_exponents,
    )


def solution(mesh):
    return jax.shard_map(
        functools.partial(on_device, mesh.shape["tensor"]),
        mesh=mesh,
        in_specs=(
            P(("groups", "req"), "tensor", None),
            P(("groups", "req"), "tensor", None, None),
            P(("groups", "req"), "tensor", None, None),
            P(("groups", "req"), None, None, None),
            P(("groups", "req")),
            P("tensor", None),
            P(("groups", "req"), "tensor"),
            P(),
            P("tensor", ("groups", "req"), None),
            P(("groups", "req"), None),
        ),
        out_specs=(P(("groups", "req"), "tensor"), P(("groups", "req"), None)),
        check_vma=False,
    )
```

```python
import functools
import math

import jax
import jax.numpy as jnp
from jax import lax
from jax.experimental import pallas as pl
from jax.experimental.pallas import tpu as pltpu
from jax.sharding import PartitionSpec as P

MESH = pl.DeviceIdType.MESH
LOW = -1e30


def power_two(exponents):
    shifted = exponents + 32
    result = jnp.full(exponents.shape, 2.0**-32, jnp.float32)
    for bit in range(6):
        is_set = (lax.shift_right_logical(shifted, bit) & 1) == 1
        result = result * jnp.where(is_set, jnp.float32(2.0 ** (2**bit)), jnp.float32(1.0))
    return result


def kernel(
    n,
    own_heads,
    kv_count,
    lengths_ref,
    q_hbm,
    k_hbm,
    v_hbm,
    fresh_hbm,
    w_hbm,
    residual_hbm,
    pexp_hbm,
    ag,
    kbuf,
    vbuf,
    wbuf,
    qbuf,
    q32,
    fresh,
    residual,
    pexp,
    groups_at,
    plim,
    mix32,
    mix_out,
    mix_in,
    stat_own,
    stat_in,
    att,
    rs_out,
    rs_in,
    state,
    k_sem,
    v_sem,
    w_sem,
    small_sem,
    own_sem,
    send_sem,
    recv_sem,
):
    me = lax.axis_index("tensor")
    rows = kbuf.shape[0]
    spots = kbuf.shape[1]
    head_size = kbuf.shape[2]
    heads = n * own_heads
    per_group = heads // kv_count
    share = wbuf.shape[2]
    half = share // 2
    block = 128
    blocks = share // block
    c = head_size ** (-0.5) / math.log(2.0)

    def partner(k):
        return lax.rem(me + k, n)

    barrier = pltpu.get_barrier_semaphore()

    @pl.loop(1, n)
    def _(k):
        pl.semaphore_signal(barrier, inc=1, device_id={"tensor": partner(k)}, device_id_type=MESH)

    own_q = pltpu.make_async_copy(q_hbm, qbuf.at[me], own_sem)
    own_q.start()
    small = [
        pltpu.make_async_copy(fresh_hbm, fresh, small_sem.at[0]),
        pltpu.make_async_copy(pexp_hbm, pexp, small_sem.at[1]),
        pltpu.make_async_copy(residual_hbm, residual, small_sem.at[2]),
    ]
    for copy in small:
        copy.start()

    def k_copy(r):
        return pltpu.make_async_copy(k_hbm.at[r], kbuf.at[r], k_sem.at[r])

    def v_copy(r):
        return pltpu.make_async_copy(v_hbm.at[r], vbuf.at[r], v_sem.at[r])

    def w_copy(j):
        return pltpu.make_async_copy(
            w_hbm.at[:, pl.ds(pl.multiple_of(j * share, share), share)], wbuf.at[j], w_sem.at[j]
        )

    for r in range(rows):
        k_copy(r).start()
        v_copy(r).start()

    @pl.loop(0, n)
    def _(k):
        w_copy(partner(k + 1)).start()

    own_q.wait()
    pl.semaphore_wait(barrier, n - 1)

    def remote(phase, src, dst, to, frm):
        return pltpu.make_async_remote_copy(
            src_ref=src,
            dst_ref=dst,
            send_sem=send_sem.at[phase, to],
            recv_sem=recv_sem.at[phase, frm],
            device_id={"tensor": to},
            device_id_type=MESH,
        )

    @pl.loop(1, n)
    def _(k):
        remote(0, qbuf.at[me], qbuf.at[me], partner(k), me).start()

    columns = lax.broadcasted_iota(jnp.int32, (heads, spots), 1)
    head_of = lax.broadcasted_iota(jnp.int32, (heads, spots), 0)
    groups_at[...] = jnp.where(
        (columns & (kv_count - 1)) == lax.shift_right_logical(head_of, per_group.bit_length() - 1), columns, 1 << 24
    )
    for copy in small:
        copy.wait()
    plimits = 448.0 * power_two(pexp[0])
    for b in range(n * blocks):
        plim[b] = jnp.broadcast_to(plimits[:, b : b + 1], (rows, block))

    @pl.loop(1, n)
    def _(k):
        src = partner(k)
        remote(0, qbuf.at[src], qbuf.at[src], src, src).wait_recv()

    for t in range(n):
        q32[:, t * own_heads : (t + 1) * own_heads, :] = (
            qbuf[t].astype(jnp.float32).reshape(rows, own_heads, head_size)
        )

    for r in range(rows):
        k_copy(r).wait()
        v_copy(r).wait()

    def score(r):
        return lax.dot_general(
            q32[r].astype(jnp.bfloat16),
            kbuf[r],
            (((1,), (1,)), ((), ())),
            preferred_element_type=jnp.float32,
        )

    def per_head(fresh_row, first):
        return jnp.concatenate(
            [
                jnp.broadcast_to(fresh_row[first + g : first + g + 1], (per_group, head_size))
                for g in range(kv_count)
            ],
            axis=0,
        )

    scores = score(0)
    for r in range(rows):
        later = score(r + 1) if r + 1 < rows else None
        fresh_row = fresh[r].astype(jnp.float32)
        fresh_score = jnp.sum(q32[r] * per_head(fresh_row, 0), axis=1, keepdims=True)
        fresh_score = jnp.where(me == 0, fresh_score, LOW)
        limit = lengths_ref[r] * kv_count - me * spots
        scores = jnp.where(groups_at[...] < limit, scores, LOW)
        top = jnp.maximum(jnp.max(scores, axis=1, keepdims=True), fresh_score)
        weights = jnp.exp2((scores - top) * c)
        own_weight = jnp.exp2((fresh_score - top) * c)
        total = jnp.sum(weights, axis=1, keepdims=True) + own_weight
        mix = jnp.dot(weights.astype(jnp.bfloat16), vbuf[r], preferred_element_type=jnp.float32)
        mix32[pl.ds(r, heads, stride=rows), :] = mix + own_weight * per_head(
            fresh_row, kv_count
        )
        stats = jnp.concatenate(
            [
                jnp.broadcast_to(top, (heads, 2 * heads)),
                jnp.broadcast_to(total, (heads, 2 * heads)),
            ],
            axis=0,
        )
        stat_own[pl.ds(r, 1), :] = jnp.transpose(stats)[0:1]
        scores = later

    piece = own_heads * rows
    for t in range(n):
        mix_out[t] = mix32[t * piece : (t + 1) * piece, :].astype(jnp.bfloat16)

    @pl.loop(1, n)
    def _(k):
        dst = partner(k)
        remote(2, stat_own, stat_in.at[me], dst, me).start()
        remote(1, mix_out.at[dst], mix_in.at[me], dst, me).start()

    stat_in[me] = stat_own[...]
    mix_in[me] = mix_out[me]

    @pl.loop(1, n)
    def _(k):
        src = partner(k)
        remote(2, stat_own, stat_in.at[src], src, src).wait_recv()
        remote(1, mix_out.at[src], mix_in.at[src], src, src).wait_recv()

    tops = [stat_in[s] for s in range(n)]
    highest = functools.reduce(jnp.maximum, tops)
    scales = [jnp.exp2((top - highest) * c) for top in tops]
    weight_sum = sum(
        pltpu.roll(tops[s], heads, 1) * scales[s] for s in range(n)
    )
    shift = lax.rem(2 * heads - me * own_heads, 2 * heads)
    inverse = 1.0 / weight_sum
    scales = [pltpu.roll(scale * inverse, shift, 1) for scale in scales]
    arrived = [mix_in[s].astype(jnp.float32) for s in range(n)]
    pieces = []
    for h in range(own_heads):
        pieces.append(
            sum(
                arrived[s][h * rows : (h + 1) * rows] * scales[s][:, h : h + 1] for s in range(n)
            )
        )
    att[...] = jnp.concatenate(pieces, axis=1).astype(jnp.bfloat16)

    step = min(512, half)

    def project(j):
        w_copy(j).wait()
        out = []
        for at in range(0, share, step):
            value = jnp.dot(
                att[...], wbuf[j, :, at : at + step], preferred_element_type=jnp.float32
            )
            limit = jnp.concatenate(
                [plim[j * blocks + at // block + b] for b in range(step // block)], axis=1
            )
            out.append(jnp.clip(value, -limit, limit))
        left = jnp.concatenate(out[: len(out) // 2], axis=1)
        right = jnp.concatenate(out[len(out) // 2 :], axis=1)
        return jnp.concatenate([left, right], axis=0).astype(jnp.bfloat16)

    @pl.loop(1, n)
    def _(k):
        dst = partner(k)
        rs_out[dst] = project(dst)
        remote(3, rs_out.at[dst], rs_in.at[me], dst, me).start()

    rs_in[me] = project(me)
    own = residual[...].astype(jnp.float32)
    total = jnp.concatenate([own[:, :half], own[:, half:]], axis=0)

    @pl.loop(1, n)
    def _(k):
        src = partner(k)
        remote(3, rs_out.at[src], rs_in.at[src], src, src).wait_recv()

    summed = rs_in[0].astype(jnp.float32)
    for s in range(1, n):
        summed = summed + rs_in[s].astype(jnp.float32)
    state[...] = (total + summed).astype(jnp.bfloat16)

    @pl.loop(1, n)
    def _(k):
        remote(4, state, ag.at[me], partner(k), me).start()

    own_state = pltpu.make_async_copy(state, ag.at[me], own_sem)
    own_state.start()

    @pl.loop(1, n)
    def _(k):
        src = partner(k)
        remote(4, state, ag.at[src], src, src).wait_recv()

    own_state.wait()

    @pl.loop(1, n)
    def _(k):
        dst = partner(k)
        remote(0, qbuf.at[me], qbuf.at[me], dst, me).wait_send()
        remote(1, mix_out.at[dst], mix_in.at[me], dst, me).wait_send()
        remote(2, stat_own, stat_in.at[me], dst, me).wait_send()
        remote(3, rs_out.at[dst], rs_in.at[me], dst, me).wait_send()
        remote(4, state, ag.at[me], dst, me).wait_send()


def norm_kernel(n, gain, nexp, ag, hidden_ref, normed_ref):
    rows = nexp.shape[0]
    half = ag.shape[2]
    share = 2 * half
    block = gain.shape[1]
    blocks = share // block
    own = ag[lax.axis_index("tensor")].astype(jnp.float32)
    hidden_ref[...] = jnp.concatenate([own[:rows], own[rows:]], axis=1).astype(jnp.bfloat16)
    squares = jnp.zeros((2 * rows, half), jnp.float32)
    for s in range(n):
        value = ag[s].astype(jnp.float32)
        squares = squares + value * value
    squares = jnp.sum(squares, axis=1, keepdims=True)
    squares = squares[:rows] + squares[rows:]
    root = lax.rsqrt(squares / (n * share) + 1e-05)
    limits = 448.0 * power_two(nexp[...])
    gains = gain[...].astype(jnp.float32)
    for s in range(n):
        value = ag[s].astype(jnp.float32)
        out = []
        for b in range(blocks):
            side, at = divmod(b * block, half)
            part = value[side * rows : (side + 1) * rows, at : at + block]
            index = s * blocks + b
            scaled = part * root * gains[index : index + 1, :]
            limit = limits[:, index : index + 1]
            out.append(jnp.clip(scaled, -limit, limit))
        normed_ref[:, s * share : (s + 1) * share] = jnp.concatenate(out, axis=1).astype(
            jnp.bfloat16
        )


def on_device(
    n,
    queries,
    key_cache,
    value_cache,
    fresh_pair,
    lengths,
    out_weight,
    residual,
    norm_gain,
    partial_exponents,
    normed_exponents,
):
    rows, own_heads, head_size = queries.shape
    positions, kv_count = key_cache.shape[1:3]
    spots = positions * kv_count
    heads = n * own_heads
    depth, width = out_weight.shape
    share = width // n
    half = share // 2
    all_blocks = normed_exponents.shape[1]
    block = width // all_blocks
    piece = rows * own_heads
    anywhere = pl.BlockSpec(memory_space=pl.ANY)
    in_vmem = pl.BlockSpec(memory_space=pltpu.VMEM)
    bf16, f32 = jnp.bfloat16, jnp.float32
    dma = pltpu.SemaphoreType.DMA
    gathered = pl.pallas_call(
        functools.partial(kernel, n, own_heads, kv_count),
        out_shape=jax.ShapeDtypeStruct((n, 2 * rows, half), bf16),
        in_specs=[pl.BlockSpec(memory_space=pltpu.SMEM)] + [anywhere] * 7,
        out_specs=anywhere,
        scratch_shapes=[
            pltpu.VMEM((rows, spots, head_size), bf16),
            pltpu.VMEM((rows, spots, head_size), bf16),
            pltpu.VMEM((n, depth, share), bf16),
            pltpu.VMEM((n, piece, head_size), bf16),
            pltpu.VMEM((rows, heads, head_size), f32),
            pltpu.VMEM((rows, 2 * kv_count, head_size), bf16),
            pltpu.VMEM((rows, share), bf16),
            pltpu.VMEM((1, rows, all_blocks), jnp.int32),
            pltpu.VMEM((heads, spots), jnp.int32),
            pltpu.VMEM((all_blocks, rows, block), f32),
            pltpu.VMEM((heads * rows, head_size), f32),
            pltpu.VMEM((n, piece, head_size), bf16),
            pltpu.VMEM((n, piece, head_size), bf16),
            pltpu.VMEM((rows, 2 * heads), f32),
            pltpu.VMEM((n, rows, 2 * heads), f32),
            pltpu.VMEM((rows, depth), bf16),
            pltpu.VMEM((n, 2 * rows, half), bf16),
            pltpu.VMEM((n, 2 * rows, half), bf16),
            pltpu.VMEM((2 * rows, half), bf16),
            dma((rows,)),
            dma((rows,)),
            dma((n,)),
            dma((3,)),
            dma,
            dma((5, n)),
            dma((5, n)),
        ],
        compiler_params=pltpu.CompilerParams(
            collective_id=0, has_side_effects=True, vmem_limit_bytes=60 * 2**20
        ),
    )(
        lengths,
        queries.reshape(piece, head_size),
        key_cache.reshape(rows, spots, head_size),
        value_cache.reshape(rows, spots, head_size),
        fresh_pair.reshape(rows, 2 * kv_count, head_size),
        out_weight,
        residual,
        partial_exponents,
    )
    return pl.pallas_call(
        functools.partial(norm_kernel, n),
        out_shape=(
            jax.ShapeDtypeStruct((rows, share), bf16),
            jax.ShapeDtypeStruct((rows, width), bf16),
        ),
        in_specs=[in_vmem] * 3,
        out_specs=(in_vmem, in_vmem),
        compiler_params=pltpu.CompilerParams(vmem_limit_bytes=60 * 2**20),
    )(norm_gain.reshape(all_blocks, block), normed_exponents, gathered)


def solution(mesh):
    return jax.shard_map(
        functools.partial(on_device, mesh.shape["tensor"]),
        mesh=mesh,
        in_specs=(
            P(("groups", "req"), "tensor", None),
            P(("groups", "req"), "tensor", None, None),
            P(("groups", "req"), "tensor", None, None),
            P(("groups", "req"), None, None, None),
            P(("groups", "req")),
            P("tensor", None),
            P(("groups", "req"), "tensor"),
            P(),
            P("tensor", ("groups", "req"), None),
            P(("groups", "req"), None),
        ),
        out_specs=(P(("groups", "req"), "tensor"), P(("groups", "req"), None)),
        check_vma=False,
    )
```

```python
import functools
import math

import jax
import jax.numpy as jnp
from jax import lax
from jax.experimental import pallas as pl
from jax.experimental.pallas import tpu as pltpu
from jax.sharding import PartitionSpec as P

MESH = pl.DeviceIdType.MESH
LOW = -1e30


def power_two(exponents):
    shifted = exponents + 32
    result = jnp.full(exponents.shape, 2.0**-32, jnp.float32)
    for bit in range(6):
        is_set = (lax.shift_right_logical(shifted, bit) & 1) == 1
        result = result * jnp.where(is_set, jnp.float32(2.0 ** (2**bit)), jnp.float32(1.0))
    return result


def kernel(
    n,
    own_heads,
    kv_count,
    lengths_ref,
    q_hbm,
    k_hbm,
    v_hbm,
    fresh_hbm,
    w_hbm,
    residual_hbm,
    pexp_hbm,
    ag,
    kbuf,
    vbuf,
    wbuf,
    qbuf,
    q32,
    fresh,
    residual,
    pexp,
    groups_at,
    plim,
    mix32,
    mix_out,
    mix_in,
    stat_own,
    stat_in,
    att,
    rs_out,
    rs_in,
    state,
    k_sem,
    v_sem,
    w_sem,
    small_sem,
    own_sem,
    send_sem,
    recv_sem,
):
    me = lax.axis_index("tensor")
    rows = kbuf.shape[0]
    spots = kbuf.shape[1]
    head_size = kbuf.shape[2]
    heads = n * own_heads
    per_group = heads // kv_count
    share = wbuf.shape[2]
    half = share // 2
    block = 128
    blocks = share // block
    c = head_size ** (-0.5) / math.log(2.0)

    parts = 2 if rows * own_heads % 32 == 0 else 1
    q_part = rows * own_heads // parts

    def partner(k):
        return lax.rem(me + k, n)

    barrier = pltpu.get_barrier_semaphore()

    @pl.loop(1, n)
    def _(k):
        pl.semaphore_signal(barrier, inc=1, device_id={"tensor": partner(k)}, device_id_type=MESH)

    own_q = pltpu.make_async_copy(q_hbm, qbuf.at[me], own_sem)
    own_q.start()
    small = [
        pltpu.make_async_copy(fresh_hbm, fresh, small_sem.at[0]),
        pltpu.make_async_copy(pexp_hbm, pexp, small_sem.at[1]),
        pltpu.make_async_copy(residual_hbm, residual, small_sem.at[2]),
    ]
    for copy in small:
        copy.start()

    def k_copy(r):
        return pltpu.make_async_copy(k_hbm.at[r], kbuf.at[r], k_sem.at[r])

    def v_copy(r):
        return pltpu.make_async_copy(v_hbm.at[r], vbuf.at[r], v_sem.at[r])

    def w_copy(j):
        return pltpu.make_async_copy(
            w_hbm.at[:, pl.ds(pl.multiple_of(j * share, share), share)], wbuf.at[j], w_sem.at[j]
        )

    for r in range(rows):
        k_copy(r).start()
        v_copy(r).start()

    @pl.loop(0, n)
    def _(k):
        w_copy(partner(k + 1)).start()

    own_q.wait()
    pl.semaphore_wait(barrier, n - 1)

    def remote(phase, src, dst, to, frm):
        return pltpu.make_async_remote_copy(
            src_ref=src,
            dst_ref=dst,
            send_sem=send_sem.at[phase, to],
            recv_sem=recv_sem.at[phase, frm],
            device_id={"tensor": to},
            device_id_type=MESH,
        )

    def q_copy(p, to, frm, slot):
        part = qbuf.at[slot, pl.ds(p * q_part, q_part)]
        return remote(0 if p == 0 else 5, part, part, to, frm)

    for p in range(parts):

        @pl.loop(1, n)
        def _(k):
            q_copy(p, partner(k), me, me).start()

    columns = lax.broadcasted_iota(jnp.int32, (heads, spots), 1)
    head_of = lax.broadcasted_iota(jnp.int32, (heads, spots), 0)
    groups_at[...] = jnp.where(
        (columns & (kv_count - 1)) == lax.shift_right_logical(head_of, per_group.bit_length() - 1), columns, 1 << 24
    )
    for copy in small:
        copy.wait()
    plimits = 448.0 * power_two(pexp[0])
    for b in range(n * blocks):
        plim[b] = jnp.broadcast_to(plimits[:, b : b + 1], (rows, block))

    for r in range(rows):
        k_copy(r).wait()
        v_copy(r).wait()

    def take_queries(p):
        @pl.loop(1, n)
        def _(k):
            src = partner(k)
            q_copy(p, src, src, src).wait_recv()

        count = rows // parts
        for t in range(n):
            q32[p * count : (p + 1) * count, t * own_heads : (t + 1) * own_heads, :] = (
                qbuf[t, p * q_part : (p + 1) * q_part]
                .astype(jnp.float32)
                .reshape(count, own_heads, head_size)
            )

    def score(r):
        return lax.dot_general(
            q32[r].astype(jnp.bfloat16),
            kbuf[r],
            (((1,), (1,)), ((), ())),
            preferred_element_type=jnp.float32,
        )

    def per_head(fresh_row, first):
        return jnp.concatenate(
            [
                jnp.broadcast_to(fresh_row[first + g : first + g + 1], (per_group, head_size))
                for g in range(kv_count)
            ],
            axis=0,
        )

    for r in range(rows):
        if r % (rows // parts) == 0:
            take_queries(r * parts // rows)
            scores = score(r)
        later = score(r + 1) if (r + 1) % (rows // parts) else None
        fresh_row = fresh[r].astype(jnp.float32)
        fresh_score = jnp.sum(q32[r] * per_head(fresh_row, 0), axis=1, keepdims=True)
        fresh_score = jnp.where(me == 0, fresh_score, LOW)
        limit = lengths_ref[r] * kv_count - me * spots
        scores = jnp.where(groups_at[...] < limit, scores, LOW)
        top = jnp.maximum(jnp.max(scores, axis=1, keepdims=True), fresh_score)
        weights = jnp.exp2((scores - top) * c)
        own_weight = jnp.exp2((fresh_score - top) * c)
        total = jnp.sum(weights, axis=1, keepdims=True) + own_weight
        mix = jnp.dot(weights.astype(jnp.bfloat16), vbuf[r], preferred_element_type=jnp.float32)
        mix32[pl.ds(r, heads, stride=rows), :] = mix + own_weight * per_head(
            fresh_row, kv_count
        )
        stats = jnp.concatenate(
            [
                jnp.broadcast_to(top, (heads, 2 * heads)),
                jnp.broadcast_to(total, (heads, 2 * heads)),
            ],
            axis=0,
        )
        stat_own[pl.ds(r, 1), :] = jnp.transpose(stats)[0:1]
        scores = later

    piece = own_heads * rows
    for t in range(n):
        mix_out[t] = mix32[t * piece : (t + 1) * piece, :].astype(jnp.bfloat16)

    @pl.loop(1, n)
    def _(k):
        dst = partner(k)
        remote(2, stat_own, stat_in.at[me], dst, me).start()
        remote(1, mix_out.at[dst], mix_in.at[me], dst, me).start()

    stat_in[me] = stat_own[...]
    mix_in[me] = mix_out[me]

    @pl.loop(1, n)
    def _(k):
        src = partner(k)
        remote(2, stat_own, stat_in.at[src], src, src).wait_recv()
        remote(1, mix_out.at[src], mix_in.at[src], src, src).wait_recv()

    tops = [stat_in[s] for s in range(n)]
    highest = functools.reduce(jnp.maximum, tops)
    scales = [jnp.exp2((top - highest) * c) for top in tops]
    weight_sum = sum(
        pltpu.roll(tops[s], heads, 1) * scales[s] for s in range(n)
    )
    shift = lax.rem(2 * heads - me * own_heads, 2 * heads)
    inverse = 1.0 / weight_sum
    scales = [pltpu.roll(scale * inverse, shift, 1) for scale in scales]
    arrived = [mix_in[s].astype(jnp.float32) for s in range(n)]
    pieces = []
    for h in range(own_heads):
        pieces.append(
            sum(
                arrived[s][h * rows : (h + 1) * rows] * scales[s][:, h : h + 1] for s in range(n)
            )
        )
    att[...] = jnp.concatenate(pieces, axis=1).astype(jnp.bfloat16)

    step = min(512, half)

    def project(j):
        w_copy(j).wait()
        out = []
        for at in range(0, share, step):
            value = jnp.dot(
                att[...], wbuf[j, :, at : at + step], preferred_element_type=jnp.float32
            )
            limit = jnp.concatenate(
                [plim[j * blocks + at // block + b] for b in range(step // block)], axis=1
            )
            out.append(jnp.clip(value, -limit, limit))
        left = jnp.concatenate(out[: len(out) // 2], axis=1)
        right = jnp.concatenate(out[len(out) // 2 :], axis=1)
        return jnp.concatenate([left, right], axis=0).astype(jnp.bfloat16)

    @pl.loop(1, n)
    def _(k):
        dst = partner(k)
        rs_out[dst] = project(dst)
        remote(3, rs_out.at[dst], rs_in.at[me], dst, me).start()

    rs_in[me] = project(me)
    own = residual[...].astype(jnp.float32)
    total = jnp.concatenate([own[:, :half], own[:, half:]], axis=0)

    @pl.loop(1, n)
    def _(k):
        src = partner(k)
        remote(3, rs_out.at[src], rs_in.at[src], src, src).wait_recv()

    summed = rs_in[0].astype(jnp.float32)
    for s in range(1, n):
        summed = summed + rs_in[s].astype(jnp.float32)
    state[...] = (total + summed).astype(jnp.bfloat16)

    @pl.loop(1, n)
    def _(k):
        remote(4, state, ag.at[me], partner(k), me).start()

    own_state = pltpu.make_async_copy(state, ag.at[me], own_sem)
    own_state.start()

    @pl.loop(1, n)
    def _(k):
        src = partner(k)
        remote(4, state, ag.at[src], src, src).wait_recv()

    own_state.wait()

    @pl.loop(1, n)
    def _(k):
        dst = partner(k)
        for p in range(parts):
            q_copy(p, dst, me, me).wait_send()
        remote(1, mix_out.at[dst], mix_in.at[me], dst, me).wait_send()
        remote(2, stat_own, stat_in.at[me], dst, me).wait_send()
        remote(3, rs_out.at[dst], rs_in.at[me], dst, me).wait_send()
        remote(4, state, ag.at[me], dst, me).wait_send()


def norm_kernel(n, gain, nexp, ag, hidden_ref, normed_ref):
    rows = nexp.shape[0]
    half = ag.shape[2]
    share = 2 * half
    block = gain.shape[1]
    blocks = share // block
    own = ag[lax.axis_index("tensor")].astype(jnp.float32)
    hidden_ref[...] = jnp.concatenate([own[:rows], own[rows:]], axis=1).astype(jnp.bfloat16)
    squares = jnp.zeros((2 * rows, half), jnp.float32)
    for s in range(n):
        value = ag[s].astype(jnp.float32)
        squares = squares + value * value
    squares = jnp.sum(squares, axis=1, keepdims=True)
    squares = squares[:rows] + squares[rows:]
    root = lax.rsqrt(squares / (n * share) + 1e-05)
    limits = 448.0 * power_two(nexp[...])
    gains = gain[...].astype(jnp.float32)
    for s in range(n):
        value = ag[s].astype(jnp.float32)
        out = []
        for b in range(blocks):
            side, at = divmod(b * block, half)
            part = value[side * rows : (side + 1) * rows, at : at + block]
            index = s * blocks + b
            scaled = part * root * gains[index : index + 1, :]
            limit = limits[:, index : index + 1]
            out.append(jnp.clip(scaled, -limit, limit))
        normed_ref[:, s * share : (s + 1) * share] = jnp.concatenate(out, axis=1).astype(
            jnp.bfloat16
        )


def on_device(
    n,
    queries,
    key_cache,
    value_cache,
    fresh_pair,
    lengths,
    out_weight,
    residual,
    norm_gain,
    partial_exponents,
    normed_exponents,
):
    rows, own_heads, head_size = queries.shape
    positions, kv_count = key_cache.shape[1:3]
    spots = positions * kv_count
    heads = n * own_heads
    depth, width = out_weight.shape
    share = width // n
    half = share // 2
    all_blocks = normed_exponents.shape[1]
    block = width // all_blocks
    piece = rows * own_heads
    anywhere = pl.BlockSpec(memory_space=pl.ANY)
    in_vmem = pl.BlockSpec(memory_space=pltpu.VMEM)
    bf16, f32 = jnp.bfloat16, jnp.float32
    dma = pltpu.SemaphoreType.DMA
    gathered = pl.pallas_call(
        functools.partial(kernel, n, own_heads, kv_count),
        out_shape=jax.ShapeDtypeStruct((n, 2 * rows, half), bf16),
        in_specs=[pl.BlockSpec(memory_space=pltpu.SMEM)] + [anywhere] * 7,
        out_specs=anywhere,
        scratch_shapes=[
            pltpu.VMEM((rows, spots, head_size), bf16),
            pltpu.VMEM((rows, spots, head_size), bf16),
            pltpu.VMEM((n, depth, share), bf16),
            pltpu.VMEM((n, piece, head_size), bf16),
            pltpu.VMEM((rows, heads, head_size), f32),
            pltpu.VMEM((rows, 2 * kv_count, head_size), bf16),
            pltpu.VMEM((rows, share), bf16),
            pltpu.VMEM((1, rows, all_blocks), jnp.int32),
            pltpu.VMEM((heads, spots), jnp.int32),
            pltpu.VMEM((all_blocks, rows, block), f32),
            pltpu.VMEM((heads * rows, head_size), f32),
            pltpu.VMEM((n, piece, head_size), bf16),
            pltpu.VMEM((n, piece, head_size), bf16),
            pltpu.VMEM((rows, 2 * heads), f32),
            pltpu.VMEM((n, rows, 2 * heads), f32),
            pltpu.VMEM((rows, depth), bf16),
            pltpu.VMEM((n, 2 * rows, half), bf16),
            pltpu.VMEM((n, 2 * rows, half), bf16),
            pltpu.VMEM((2 * rows, half), bf16),
            dma((rows,)),
            dma((rows,)),
            dma((n,)),
            dma((3,)),
            dma,
            dma((6, n)),
            dma((6, n)),
        ],
        compiler_params=pltpu.CompilerParams(
            collective_id=0, has_side_effects=True, vmem_limit_bytes=60 * 2**20
        ),
    )(
        lengths,
        queries.reshape(piece, head_size),
        key_cache.reshape(rows, spots, head_size),
        value_cache.reshape(rows, spots, head_size),
        fresh_pair.reshape(rows, 2 * kv_count, head_size),
        out_weight,
        residual,
        partial_exponents,
    )
    return pl.pallas_call(
        functools.partial(norm_kernel, n),
        out_shape=(
            jax.ShapeDtypeStruct((rows, share), bf16),
            jax.ShapeDtypeStruct((rows, width), bf16),
        ),
        in_specs=[in_vmem] * 3,
        out_specs=(in_vmem, in_vmem),
        compiler_params=pltpu.CompilerParams(vmem_limit_bytes=60 * 2**20),
    )(norm_gain.reshape(all_blocks, block), normed_exponents, gathered)


def solution(mesh):
    return jax.shard_map(
        functools.partial(on_device, mesh.shape["tensor"]),
        mesh=mesh,
        in_specs=(
            P(("groups", "req"), "tensor", None),
            P(("groups", "req"), "tensor", None, None),
            P(("groups", "req"), "tensor", None, None),
            P(("groups", "req"), None, None, None),
            P(("groups", "req")),
            P("tensor", None),
            P(("groups", "req"), "tensor"),
            P(),
            P("tensor", ("groups", "req"), None),
            P(("groups", "req"), None),
        ),
        out_specs=(P(("groups", "req"), "tensor"), P(("groups", "req"), None)),
        check_vma=False,
    )
```
